32 devices in a mesh: date: 4 (over y, core), space: 8 (over z, x).
Axes of the slice: x: 2, y: 2, z: 4, core: 2. Of those that a mesh axis runs over, the one named last changes fastest.
Arguments:
- stack: float32 [2, 28, 64, 1024], P(None, 'date', 'space'), may hold values from -6 to 6
Outputs:
- coherence: float32 [14, 28, 64, 1024], P(None, None, 'space', 'date')
The draws below stay inside these ranges and needn't reach their ends.
All inputs are finite; a program needn't handle non-finite values.
Results may differ from the reference program's by a relative error of at most 0.000068.
Values sent between devices are 32-bit elements; how exact they have to be, the bound alone decides.
A program may use at most 64 MiB of HBM per device.

```python
import jax
import jax.numpy as jnp
from jax import lax

DATES = 28
LAGS = 14
WIN_AZ = 11
WIN_RG = 23
AZ = 64
RG = 1024


def shard_levels(stream_key, dims, cuts, smallest, top_value):
    def one(axis_at, shards_of):
        heights = jax.random.uniform(jax.random.fold_in(jax.random.fold_in(stream_key, 6), axis_at), (shards_of,), jnp.float32, smallest / len(cuts), top_value / len(cuts))
        return jnp.repeat(jnp.exp(heights), dims[axis_at] // shards_of).reshape((-1,) + (1,) * (len(dims) - axis_at - 1))

    loudness = one(*cuts[0])
    for cut in cuts[1:]:
        loudness = loudness * one(*cut)
    return loudness


def bell_draw(key, dims, deviation, most, pieces=(), kind=jnp.bfloat16):
    entries = jax.random.normal(key, dims, jnp.float32) * deviation
    if len(pieces) > 0:
        entries = shard_levels(key, dims, pieces, -0.22, 0.18) * entries
    return jnp.clip(entries, min=-most, max=most).astype(kind)


def setup_inputs(seed: int = 0) -> dict:
    key_of = jax.random.split(jax.random.key(seed), 2)
    return {
        "stack": bell_draw(key_of[0], (2, DATES, AZ, RG), 1.0, 6.0, ((1, 4), (2, 8)), jnp.float32),
    }


def boxcar(values):
    half_az = WIN_AZ // 2
    half_rg = WIN_RG // 2
    rows = values.shape[-2]
    cols = values.shape[-1]
    padded = jnp.pad(values, ((0, 0), (half_az, half_az), (half_rg, half_rg)))
    summed = padded[:, 0:rows, :]
    for offset in range(1, WIN_AZ):
        summed = summed + padded[:, offset:offset + rows, :]
    total = summed[:, :, 0:cols]
    for offset in range(1, WIN_RG):
        total = total + summed[:, :, offset:offset + cols]
    return total

def reference(stack):
    real_part = stack[0]
    imag_part = stack[1]
    power = boxcar(real_part * real_part + imag_part * imag_part)

    def one_lag(lag):
        shift = lag + 1
        real_other = jnp.roll(real_part, -shift, axis=0)
        imag_other = jnp.roll(imag_part, -shift, axis=0)
        power_other = jnp.roll(power, -shift, axis=0)
        cross_re = boxcar(real_part * real_other + imag_part * imag_other)
        cross_im = boxcar(imag_part * real_other - real_part * imag_other)
        return jnp.sqrt(cross_re * cross_re + cross_im * cross_im) / jnp.sqrt(power * power_other)
    return lax.map(one_lag, jnp.arange(LAGS, dtype=jnp.int32))
```

```python
import functools

import jax
import jax.numpy as jnp
from jax import lax
from jax.experimental import pallas as pl
from jax.experimental.pallas import tpu as pltpu
from jax.sharding import PartitionSpec as P

F32 = jnp.float32
BF16 = jnp.bfloat16
HALF_AZ = 5
HALF_RG = 11
LANES = 128
MESH = pl.DeviceIdType.MESH
OWN, ABOVE, BELOW = 0, 9, 15
PLANES = 21


def pack_tile(tiles, snd, groups, rows, dates):
    lane = lax.broadcasted_iota(jnp.int32, (8, LANES), 1)

    per = tiles.shape[0] // groups

    def plane(l, c, r):
        return snd[l // per, 1 + r, c * per + l % per]

    for l in range(tiles.shape[0]):
        for c in range(2):
            block = tiles[l, c * dates * rows:(c * dates + 8) * rows].reshape(8, rows, LANES)
            block = jnp.swapaxes(block, 0, 1)
            for r in range(rows):
                snd[l // per, 1 + r, c * per + l % per] = block[r]
    for d in range(groups):
        for c in range(2):
            for t in range(2):
                tail = jnp.zeros((8, LANES), F32)
                for q in range(4):
                    at = 32 * q
                    if d > 0:
                        left = pltpu.roll(plane(d * per - 1, c, 4 * t + q), (at + HALF_RG) % LANES, 1)
                        tail = jnp.where((lane >= at) & (lane < at + HALF_RG), left, tail)
                    if d < groups - 1:
                        right = plane((d + 1) * per, c, 4 * t + q)
                        right = pltpu.roll(right, at + HALF_RG, 1)
                        tail = jnp.where((lane >= at + HALF_RG) & (lane < at + 2 * HALF_RG), right, tail)
                snd[d, 0, 2 * c + t] = tail
                snd[d, 9, 2 * c + t] = tail


def exchange(groups, spaces, rows, dates, x_ref, rcv, tiles, snd, in_sem, self_sem, send_sem, recv_sem):
    g = lax.axis_index("date")
    s = lax.axis_index("space")
    loads = []
    for l in range(tiles.shape[0]):
        n = x_ref.shape[0]
        loads.append(
            pltpu.make_async_copy(
                x_ref.at[:, pl.ds(l * LANES, LANES)], tiles.at[l, pl.ds(0, n)], in_sem.at[l]
            )
        )
        loads[-1].start()
        tiles[l, pl.ds(n, 16)] = jnp.zeros((16, LANES), F32)

    up = lax.rem(s + spaces - 1, spaces)
    down = lax.rem(s + 1, spaces)
    barrier = pltpu.get_barrier_semaphore()

    def greet(d, to):
        pl.semaphore_signal(barrier, inc=1, device_id={"date": d, "space": to}, device_id_type=MESH)

    for off in range(groups):
        d = lax.rem(g + off, groups)
        greet(d, up)
        greet(d, down)
        if off:
            greet(d, s)
    for copy in loads:
        copy.wait()
    pack_tile(tiles, snd, groups, rows, dates)
    pl.semaphore_wait(barrier, 3 * groups - 1)

    def copy_of(kind, off, to, first, count, at, source):
        d = lax.rem(g + off, groups)
        return pltpu.make_async_remote_copy(
            src_ref=snd.at[d, pl.ds(first, count)],
            dst_ref=rcv.at[source, pl.ds(at, count)],
            send_sem=send_sem.at[kind * groups + off],
            recv_sem=recv_sem.at[kind * groups + off],
            device_id={"date": d, "space": to},
            device_id_type=MESH,
        )

    sent = []
    for off in (2, 3, 1, 0):
        sent.append((0, off, up, 0, 6, BELOW))
        sent.append((1, off, down, 4, 6, ABOVE))
        if off:
            sent.append((2, off, s, 0, 9, OWN))
    for args in sent:
        copy_of(*args, g).start()
    keep = pltpu.make_async_copy(snd.at[g, pl.ds(0, 9)], rcv.at[g, pl.ds(OWN, 9)], self_sem)
    keep.start()
    keep.wait()
    for args in sent:
        copy_of(*args, lax.rem(g + groups - args[1], groups)).wait_recv()
    for args in sent:
        copy_of(*args, g).wait_send()

    @pl.when(s == 0)
    def _():
        rcv[:, ABOVE:ABOVE + 6] = jnp.zeros((groups, 6) + rcv.shape[2:], F32)

    @pl.when(s == spaces - 1)
    def _():
        rcv[:, BELOW:BELOW + 6] = jnp.zeros((groups, 6) + rcv.shape[2:], F32)


def source_of(row):
    if row < HALF_AZ:
        own = row + 3
        return ABOVE + row, ABOVE + 5, own // 4, own % 4
    if row < HALF_AZ + 8:
        own = row - HALF_AZ
        return OWN + 1 + own, OWN, own // 4, own % 4
    own = row - HALF_AZ - 8
    return BELOW + 1 + own, BELOW, own // 4, own % 4


def window(p):
    suffix = [None] * 8
    suffix[7] = (p[7] + p[8]) + (p[9] + p[10])
    for r in range(6, -1, -1):
        suffix[r] = suffix[r + 1] + p[r]
    out = [suffix[0]]
    prefix = p[11]
    for r in range(1, 8):
        out.append(suffix[r] + prefix)
        if r < 7:
            prefix = prefix + p[11 + r]
    return out


def split(v):
    high = v.astype(BF16).astype(F32)
    return high, v - high


def unpack(rcv, main, tail, wide, groups, dates):
    lane = lax.broadcasted_iota(jnp.int32, (24, LANES), 1)
    for c in range(2):
        for row in range(18):
            plane = source_of(row)[0]
            for l in range(2):
                for h in range(2 * groups):
                    main[c, row, l, pl.ds(dates * h, dates)] = rcv[h % groups, plane, 2 * c + l, 0:dates]
        for n, plane in enumerate((OWN, ABOVE + 5, BELOW)):
            for t in range(2):
                for h in range(2 * groups):
                    wide[c, n, t, pl.ds(dates * h, dates)] = rcv[h % groups, plane, 2 * c + t, 0:dates]
        for row in range(18):
            _, plane, t, q = source_of(row)
            n = (OWN, ABOVE + 5, BELOW).index(plane)
            packed = None
            for b in range(4):
                part = wide[c, n, t, pl.ds(8 * b, 24)]
                if b != q:
                    part = pltpu.roll(part, (32 * (b - q)) % LANES, 1)
                packed = part if packed is None else jnp.where(lane >= 32 * b, part, packed)
            tail[c, row] = packed


def fill_lhs(shift, main, tail, lhs, power_only):
    comps = 1 if power_only else 2
    for l in range(2):
        for b in range(2):
            first, second = [], []
            for row in range(18):
                a = main[0, row, l, pl.ds(16 * b, 16)]
                e = main[1, row, l, pl.ds(16 * b, 16)]
                if power_only:
                    first.append(a * a + e * e)
                else:
                    ao = main[0, row, l, pl.ds(16 * b + shift, 16)]
                    eo = main[1, row, l, pl.ds(16 * b + shift, 16)]
                    first.append(a * ao + e * eo)
                    second.append(e * ao - a * eo)
            for c, planes in enumerate((first, second)[:comps]):
                for r, v in enumerate(window(planes)):
                    high, low = split(v)
                    at = pl.ds(256 * c + 32 * r + 16 * b, 16)
                    lhs[at, LANES * l:LANES * (l + 1)] = high.astype(BF16)
                    lhs[at, LANES * (2 + l):LANES * (3 + l)] = low.astype(BF16)
    first, second = [], []
    for row in range(18):
        a = tail[0, row, 0:8]
        e = tail[1, row, 0:8]
        if power_only:
            first.append(a * a + e * e)
        else:
            ao = tail[0, row, pl.ds(shift, 8)]
            eo = tail[1, row, pl.ds(shift, 8)]
            first.append(a * ao + e * eo)
            second.append(e * ao - a * eo)
    block = lax.broadcasted_iota(jnp.int32, (8, LANES), 1) // 32
    for c, planes in enumerate((first, second)[:comps]):
        for r, v in enumerate(window(planes)):
            for n, part in enumerate(split(v)):
                for b in range(2):
                    both = jnp.concatenate(
                        [jnp.where(block == 2 * b + h, part, 0.0) for h in range(2)], axis=0
                    )
                    lhs[pl.ds(256 * c + 32 * r + 16 * b, 16), LANES * (4 + n):LANES * (5 + n)] = both.astype(BF16)


def pairs(groups, dates, rcv, out, main, tail, wide, lhs, res, inv, band):
    k = pl.program_id(0)
    total = groups * dates

    @pl.when(k == 0)
    def _():
        i = lax.broadcasted_iota(jnp.int32, (256, 256), 0)
        o = lax.broadcasted_iota(jnp.int32, (256, 256), 1)
        centre = jnp.where((i >= o - HALF_RG) & (i <= o + HALF_RG), 1.0, 0.0).astype(BF16)
        it = lax.broadcasted_iota(jnp.int32, (128, 256), 0) % 32
        ot = lax.broadcasted_iota(jnp.int32, (128, 256), 1)
        col = jnp.where(it < HALF_RG, it - HALF_RG, 256 + it - HALF_RG)
        edge = jnp.where(
            (it < 2 * HALF_RG) & (col >= ot - HALF_RG) & (col <= ot + HALF_RG), 1.0, 0.0
        ).astype(BF16)
        band[0:256] = centre
        band[256:512] = centre
        band[512:640] = edge
        band[640:768] = edge
        unpack(rcv, main, tail, wide, groups, dates)
        fill_lhs(0, main, tail, lhs, True)
        power = jnp.dot(lhs[0:256], band[...], preferred_element_type=F32)
        for l in range(2):
            res[0, l, 0:256] = lax.rsqrt(power[:, LANES * l:LANES * (l + 1)])
        for d in range(total):
            for l in range(2):
                inv[d, :, LANES * l:LANES * (l + 1)] = res[0, l, pl.ds(d, 8, stride=32), :]

    fill_lhs(k + 1, main, tail, lhs, False)
    both = jnp.dot(lhs[...], band[...], preferred_element_type=F32)
    for c in range(2):
        for l in range(2):
            res[c, l, 0:256] = both[256 * c:256 * (c + 1), LANES * l:LANES * (l + 1)]
    for d in range(total):
        other = lax.rem(d + k + 1, total)
        for l in range(2):
            cols = slice(LANES * l, LANES * (l + 1))
            re = res[0, l, pl.ds(d, 8, stride=32), :]
            im = res[1, l, pl.ds(d, 8, stride=32), :]
            out[0, d, :, cols] = jnp.sqrt(re * re + im * im) * (inv[d, :, cols] * inv[other, :, cols])


def body(groups, spaces, stack):
    _, dates, rows, cols = stack.shape
    n_tiles = cols // LANES
    lags = groups * dates // 2
    flat = stack.reshape(2 * dates * rows, cols)
    rcv = pl.pallas_call(
        functools.partial(exchange, groups, spaces, rows, dates),
        out_shape=jax.ShapeDtypeStruct((groups, PLANES, 4, 8, LANES), F32),
        in_specs=[pl.BlockSpec(memory_space=pl.ANY)],
        out_specs=pl.BlockSpec(memory_space=pltpu.VMEM),
        scratch_shapes=[
            pltpu.VMEM((n_tiles, 2 * dates * rows + 16, LANES), F32),
            pltpu.VMEM((groups, 10, 4, 8, LANES), F32),
            pltpu.SemaphoreType.DMA((n_tiles,)),
            pltpu.SemaphoreType.DMA,
            pltpu.SemaphoreType.DMA((3 * groups,)),
            pltpu.SemaphoreType.DMA((3 * groups,)),
        ],
        compiler_params=pltpu.CompilerParams(
            collective_id=0, has_side_effects=True, vmem_limit_bytes=24 << 20
        ),
        name="exchange",
    )(flat)
    width = cols // groups
    return pl.pallas_call(
        functools.partial(pairs, groups, dates),
        grid=(lags,),
        out_shape=jax.ShapeDtypeStruct((lags, groups * dates, rows, width), F32),
        in_specs=[pl.BlockSpec(rcv.shape, lambda k: (0,) * 5)],
        out_specs=pl.BlockSpec((1, groups * dates, rows, width), lambda k: (k, 0, 0, 0)),
        scratch_shapes=[
            pltpu.VMEM((2, 18, 2, 56, LANES), F32),
            pltpu.VMEM((2, 18, 24, LANES), F32),
            pltpu.VMEM((2, 3, 2, 56, LANES), F32),
            pltpu.VMEM((512, 6 * LANES), BF16),
            pltpu.VMEM((2, 2, 288, LANES), F32),
            pltpu.VMEM((groups * dates, rows, width), F32),
            pltpu.VMEM((6 * LANES, 256), BF16),
        ],
        compiler_params=pltpu.CompilerParams(vmem_limit_bytes=32 << 20),
        name="pairs",
    )(rcv)


def solution(mesh):
    groups, spaces = mesh.shape["date"], mesh.shape["space"]
    return jax.shard_map(
        functools.partial(body, groups, spaces),
        mesh=mesh,
        in_specs=(P(None, "date", "space", None),),
        out_specs=P(None, None, "space", "date"),
        check_vma=False,
    )
```

```python
import functools

import jax
import jax.numpy as jnp
from jax import lax
from jax.experimental import pallas as pl
from jax.experimental.pallas import tpu as pltpu
from jax.sharding import PartitionSpec as P

F32 = jnp.float32
BF16 = jnp.bfloat16
HALF_AZ = 5
HALF_RG = 11
LANES = 128
MESH = pl.DeviceIdType.MESH
OWN, ABOVE, BELOW = 0, 9, 15
PLANES = 21


def pack_tile(tiles, snd, groups, rows, dates):
    lane = lax.broadcasted_iota(jnp.int32, (8, LANES), 1)

    per = tiles.shape[0] // groups

    def plane(l, c, r):
        return snd[l // per, 1 + r, c * per + l % per]

    for l in range(tiles.shape[0]):
        for c in range(2):
            block = tiles[l, c * dates * rows:(c * dates + 8) * rows].reshape(8, rows, LANES)
            block = jnp.swapaxes(block, 0, 1)
            for r in range(rows):
                snd[l // per, 1 + r, c * per + l % per] = block[r]
    for d in range(groups):
        for c in range(2):
            for t in range(2):
                tail = jnp.zeros((8, LANES), F32)
                for q in range(4):
                    at = 32 * q
                    if d > 0:
                        left = pltpu.roll(plane(d * per - 1, c, 4 * t + q), (at + HALF_RG) % LANES, 1)
                        tail = jnp.where((lane >= at) & (lane < at + HALF_RG), left, tail)
                    if d < groups - 1:
                        right = plane((d + 1) * per, c, 4 * t + q)
                        right = pltpu.roll(right, at + HALF_RG, 1)
                        tail = jnp.where((lane >= at + HALF_RG) & (lane < at + 2 * HALF_RG), right, tail)
                snd[d, 0, 2 * c + t] = tail
                snd[d, 9, 2 * c + t] = tail


def exchange(groups, spaces, rows, dates, x_ref, rcv, tiles, snd, in_sem, self_sem, send_sem, recv_sem):
    g = lax.axis_index("date")
    s = lax.axis_index("space")
    loads = []
    for l in range(tiles.shape[0]):
        n = x_ref.shape[0]
        loads.append(
            pltpu.make_async_copy(
                x_ref.at[:, pl.ds(l * LANES, LANES)], tiles.at[l, pl.ds(0, n)], in_sem.at[l]
            )
        )
        loads[-1].start()
        tiles[l, pl.ds(n, 16)] = jnp.zeros((16, LANES), F32)

    up = lax.rem(s + spaces - 1, spaces)
    down = lax.rem(s + 1, spaces)
    barrier = pltpu.get_barrier_semaphore()

    def greet(d, to):
        pl.semaphore_signal(barrier, inc=1, device_id={"date": d, "space": to}, device_id_type=MESH)

    for off in range(groups):
        d = lax.rem(g + off, groups)
        greet(d, up)
        greet(d, down)
        if off:
            greet(d, s)
    for copy in loads:
        copy.wait()
    pack_tile(tiles, snd, groups, rows, dates)
    pl.semaphore_wait(barrier, 3 * groups - 1)

    def copy_of(kind, off, to, first, count, at, source):
        d = lax.rem(g + off, groups)
        return pltpu.make_async_remote_copy(
            src_ref=snd.at[d, pl.ds(first, count)],
            dst_ref=rcv.at[source, pl.ds(at, count)],
            send_sem=send_sem.at[kind * groups + off],
            recv_sem=recv_sem.at[kind * groups + off],
            device_id={"date": d, "space": to},
            device_id_type=MESH,
        )

    sent = []
    for off in (2, 3, 1, 0):
        sent.append((0, off, up, 0, 6, BELOW))
        sent.append((1, off, down, 4, 6, ABOVE))
        if off:
            sent.append((2, off, s, 0, 9, OWN))
    for args in sent:
        copy_of(*args, g).start()
    keep = pltpu.make_async_copy(snd.at[g, pl.ds(0, 9)], rcv.at[g, pl.ds(OWN, 9)], self_sem)
    keep.start()
    keep.wait()
    for args in sent:
        copy_of(*args, lax.rem(g + groups - args[1], groups)).wait_recv()
    for args in sent:
        copy_of(*args, g).wait_send()

    @pl.when(s == 0)
    def _():
        rcv[:, ABOVE:ABOVE + 6] = jnp.zeros((groups, 6) + rcv.shape[2:], F32)

    @pl.when(s == spaces - 1)
    def _():
        rcv[:, BELOW:BELOW + 6] = jnp.zeros((groups, 6) + rcv.shape[2:], F32)


def source_of(row):
    if row < HALF_AZ:
        own = row + 3
        return ABOVE + row, ABOVE + 5, own // 4, own % 4
    if row < HALF_AZ + 8:
        own = row - HALF_AZ
        return OWN + 1 + own, OWN, own // 4, own % 4
    own = row - HALF_AZ - 8
    return BELOW + 1 + own, BELOW, own // 4, own % 4


def window(p):
    suffix = [None] * 8
    suffix[7] = (p[7] + p[8]) + (p[9] + p[10])
    for r in range(6, -1, -1):
        suffix[r] = suffix[r + 1] + p[r]
    out = [suffix[0]]
    prefix = p[11]
    for r in range(1, 8):
        out.append(suffix[r] + prefix)
        if r < 7:
            prefix = prefix + p[11 + r]
    return out


def split(v):
    high = v.astype(BF16).astype(F32)
    return high, v - high


def unpack(rcv, main, tail, wide, groups, dates):
    lane = lax.broadcasted_iota(jnp.int32, (24, LANES), 1)
    for c in range(2):
        for row in range(18):
            plane = source_of(row)[0]
            for l in range(2):
                for h in range(2 * groups):
                    main[c, row, l, pl.ds(dates * h, dates)] = rcv[h % groups, plane, 2 * c + l, 0:dates]
        for n, plane in enumerate((OWN, ABOVE + 5, BELOW)):
            for t in range(2):
                for h in range(2 * groups):
                    wide[c, n, t, pl.ds(dates * h, dates)] = rcv[h % groups, plane, 2 * c + t, 0:dates]
        for row in range(18):
            _, plane, t, q = source_of(row)
            n = (OWN, ABOVE + 5, BELOW).index(plane)
            packed = None
            for b in range(4):
                part = wide[c, n, t, pl.ds(8 * b, 24)]
                if b != q:
                    part = pltpu.roll(part, (32 * (b - q)) % LANES, 1)
                packed = part if packed is None else jnp.where(lane >= 32 * b, part, packed)
            tail[c, row] = packed


def fill_lhs(shift, main, tail, lhs, power_only):
    comps = 1 if power_only else 2
    for l in range(2):
        for b in range(2):
            first, second = [], []
            for row in range(18):
                a = main[0, row, l, pl.ds(16 * b, 16)]
                e = main[1, row, l, pl.ds(16 * b, 16)]
                if power_only:
                    first.append(a * a + e * e)
                else:
                    ao = main[0, row, l, pl.ds(16 * b + shift, 16)]
                    eo = main[1, row, l, pl.ds(16 * b + shift, 16)]
                    first.append(a * ao + e * eo)
                    second.append(e * ao - a * eo)
            for c, planes in enumerate((first, second)[:comps]):
                for r, v in enumerate(window(planes)):
                    high, low = split(v)
                    at = pl.ds(256 * c + 32 * r + 16 * b, 16)
                    lhs[at, LANES * l:LANES * (l + 1)] = high.astype(BF16)
                    lhs[at, LANES * (2 + l):LANES * (3 + l)] = low.astype(BF16)
    first, second = [], []
    for row in range(18):
        a = tail[0, row, 0:8]
        e = tail[1, row, 0:8]
        if power_only:
            first.append(a * a + e * e)
        else:
            ao = tail[0, row, pl.ds(shift, 8)]
            eo = tail[1, row, pl.ds(shift, 8)]
            first.append(a * ao + e * eo)
            second.append(e * ao - a * eo)
    block = lax.broadcasted_iota(jnp.int32, (8, LANES), 1) // 32
    for c, planes in enumerate((first, second)[:comps]):
        for r, v in enumerate(window(planes)):
            for n, part in enumerate(split(v)):
                for b in range(2):
                    both = jnp.concatenate(
                        [jnp.where(block == 2 * b + h, part, 0.0) for h in range(2)], axis=0
                    )
                    lhs[pl.ds(256 * c + 32 * r + 16 * b, 16), LANES * (4 + n):LANES * (5 + n)] = both.astype(BF16)


def pairs(groups, dates, rcv, out, main, tail, wide, lhs, lhs_b, res, res_b, inv, band):
    k = pl.program_id(0)
    total = groups * dates

    @pl.when(k == 0)
    def _():
        i = lax.broadcasted_iota(jnp.int32, (256, 256), 0)
        o = lax.broadcasted_iota(jnp.int32, (256, 256), 1)
        centre = jnp.where((i >= o - HALF_RG) & (i <= o + HALF_RG), 1.0, 0.0).astype(BF16)
        it = lax.broadcasted_iota(jnp.int32, (128, 256), 0) % 32
        ot = lax.broadcasted_iota(jnp.int32, (128, 256), 1)
        col = jnp.where(it < HALF_RG, it - HALF_RG, 256 + it - HALF_RG)
        edge = jnp.where(
            (it < 2 * HALF_RG) & (col >= ot - HALF_RG) & (col <= ot + HALF_RG), 1.0, 0.0
        ).astype(BF16)
        band[0:256] = centre
        band[256:512] = centre
        band[512:640] = edge
        band[640:768] = edge
        unpack(rcv, main, tail, wide, groups, dates)
        fill_lhs(0, main, tail, lhs, True)
        power = jnp.dot(lhs[0:256], band[...], preferred_element_type=F32)
        for l in range(2):
            res[0, l, 0:256] = lax.rsqrt(power[:, LANES * l:LANES * (l + 1)])
        for d in range(total):
            for l in range(2):
                inv[d, :, LANES * l:LANES * (l + 1)] = res[0, l, pl.ds(d, 8, stride=32), :]

    for n, (left, sums) in enumerate(((lhs, res), (lhs_b, res_b))):
        fill_lhs(2 * k + n + 1, main, tail, left, False)
        both = jnp.dot(left[...], band[...], preferred_element_type=F32)
        for c in range(2):
            for l in range(2):
                sums[c, l, 0:256] = both[256 * c:256 * (c + 1), LANES * l:LANES * (l + 1)]
    for n, sums in enumerate((res, res_b)):
        for d in range(total):
            other = lax.rem(d + 2 * k + n + 1, total)
            for l in range(2):
                cols = slice(LANES * l, LANES * (l + 1))
                re = sums[0, l, pl.ds(d, 8, stride=32), :]
                im = sums[1, l, pl.ds(d, 8, stride=32), :]
                out[n, d, :, cols] = jnp.sqrt(re * re + im * im) * (inv[d, :, cols] * inv[other, :, cols])


def body(groups, spaces, stack):
    _, dates, rows, cols = stack.shape
    n_tiles = cols // LANES
    lags = groups * dates // 2
    flat = stack.reshape(2 * dates * rows, cols)
    rcv = pl.pallas_call(
        functools.partial(exchange, groups, spaces, rows, dates),
        out_shape=jax.ShapeDtypeStruct((groups, PLANES, 4, 8, LANES), F32),
        in_specs=[pl.BlockSpec(memory_space=pl.ANY)],
        out_specs=pl.BlockSpec(memory_space=pltpu.VMEM),
        scratch_shapes=[
            pltpu.VMEM((n_tiles, 2 * dates * rows + 16, LANES), F32),
            pltpu.VMEM((groups, 10, 4, 8, LANES), F32),
            pltpu.SemaphoreType.DMA((n_tiles,)),
            pltpu.SemaphoreType.DMA,
            pltpu.SemaphoreType.DMA((3 * groups,)),
            pltpu.SemaphoreType.DMA((3 * groups,)),
        ],
        compiler_params=pltpu.CompilerParams(
            collective_id=0, has_side_effects=True, vmem_limit_bytes=24 << 20
        ),
        name="exchange",
    )(flat)
    width = cols // groups
    return pl.pallas_call(
        functools.partial(pairs, groups, dates),
        grid=(lags // 2,),
        out_shape=jax.ShapeDtypeStruct((lags, groups * dates, rows, width), F32),
        in_specs=[pl.BlockSpec(rcv.shape, lambda k: (0,) * 5)],
        out_specs=pl.BlockSpec((2, groups * dates, rows, width), lambda k: (k, 0, 0, 0)),
        scratch_shapes=[
            pltpu.VMEM((2, 18, 2, 56, LANES), F32),
            pltpu.VMEM((2, 18, 24, LANES), F32),
            pltpu.VMEM((2, 3, 2, 56, LANES), F32),
            pltpu.VMEM((512, 6 * LANES), BF16),
            pltpu.VMEM((512, 6 * LANES), BF16),
            pltpu.VMEM((2, 2, 288, LANES), F32),
            pltpu.VMEM((2, 2, 288, LANES), F32),
            pltpu.VMEM((groups * dates, rows, width), F32),
            pltpu.VMEM((6 * LANES, 256), BF16),
        ],
        compiler_params=pltpu.CompilerParams(vmem_limit_bytes=32 << 20),
        name="pairs",
    )(rcv)


def solution(mesh):
    groups, spaces = mesh.shape["date"], mesh.shape["space"]
    return jax.shard_map(
        functools.partial(body, groups, spaces),
        mesh=mesh,
        in_specs=(P(None, "date", "space", None),),
        out_specs=P(None, None, "space", "date"),
        check_vma=False,
    )
```

```python
import functools

import jax
import jax.numpy as jnp
from jax import lax
from jax.experimental import pallas as pl
from jax.experimental.pallas import tpu as pltpu
from jax.sharding import PartitionSpec as P

F32 = jnp.float32
BF16 = jnp.bfloat16
HALF_AZ = 5
HALF_RG = 11
LANES = 128
MESH = pl.DeviceIdType.MESH
OWN, ABOVE, BELOW = 0, 9, 15
PLANES = 21


def pack_tile(tiles, snd, groups, rows, dates):
    lane = lax.broadcasted_iota(jnp.int32, (8, LANES), 1)

    per = tiles.shape[0] // groups

    def plane(l, c, r):
        return snd[l // per, 1 + r, c * per + l % per]

    for l in range(tiles.shape[0]):
        for c in range(2):
            block = tiles[l, c * dates * rows:(c * dates + 8) * rows].reshape(8, rows, LANES)
            block = jnp.swapaxes(block, 0, 1)
            for r in range(rows):
                snd[l // per, 1 + r, c * per + l % per] = block[r]
    for d in range(groups):
        for c in range(2):
            for t in range(2):
                tail = jnp.zeros((8, LANES), F32)
                for q in range(4):
                    at = 32 * q
                    if d > 0:
                        left = pltpu.roll(plane(d * per - 1, c, 4 * t + q), (at + HALF_RG) % LANES, 1)
                        tail = jnp.where((lane >= at) & (lane < at + HALF_RG), left, tail)
                    if d < groups - 1:
                        right = plane((d + 1) * per, c, 4 * t + q)
                        right = pltpu.roll(right, at + HALF_RG, 1)
                        tail = jnp.where((lane >= at + HALF_RG) & (lane < at + 2 * HALF_RG), right, tail)
                snd[d, 0, 2 * c + t] = tail
                snd[d, 9, 2 * c + t] = tail


def exchange(groups, spaces, rows, dates, x_ref, rcv, tiles, snd, in_sem, self_sem, send_sem, recv_sem):
    g = lax.axis_index("date")
    s = lax.axis_index("space")
    loads = []
    for l in range(tiles.shape[0]):
        n = x_ref.shape[0]
        loads.append(
            pltpu.make_async_copy(
                x_ref.at[:, pl.ds(l * LANES, LANES)], tiles.at[l, pl.ds(0, n)], in_sem.at[l]
            )
        )
        loads[-1].start()
        tiles[l, pl.ds(n, 16)] = jnp.zeros((16, LANES), F32)

    up = lax.rem(s + spaces - 1, spaces)
    down = lax.rem(s + 1, spaces)
    barrier = pltpu.get_barrier_semaphore()

    def greet(d, to):
        pl.semaphore_signal(barrier, inc=1, device_id={"date": d, "space": to}, device_id_type=MESH)

    for off in range(groups):
        d = lax.rem(g + off, groups)
        greet(d, up)
        greet(d, down)
        if off:
            greet(d, s)
    for copy in loads:
        copy.wait()
    pack_tile(tiles, snd, groups, rows, dates)
    pl.semaphore_wait(barrier, 3 * groups - 1)

    def copy_of(kind, off, to, first, count, at, source):
        d = lax.rem(g + off, groups)
        return pltpu.make_async_remote_copy(
            src_ref=snd.at[d, pl.ds(first, count)],
            dst_ref=rcv.at[source, pl.ds(at, count)],
            send_sem=send_sem.at[kind * groups + off],
            recv_sem=recv_sem.at[kind * groups + off],
            device_id={"date": d, "space": to},
            device_id_type=MESH,
        )

    sent = []
    for off in (2, 3, 1, 0):
        sent.append((0, off, up, 0, 6, BELOW))
        sent.append((1, off, down, 4, 6, ABOVE))
        if off:
            sent.append((2, off, s, 0, 9, OWN))
    def each(use):
        for kind, there in ((0, s > 0), (1, s < spaces - 1)):
            @pl.when(there)
            def _():
                for args in sent:
                    if args[0] == kind:
                        use(kind, args)
        for args in sent:
            if args[0] == 2:
                use(2, args)

    each(lambda kind, args: copy_of(*args, g).start())
    keep = pltpu.make_async_copy(snd.at[g, pl.ds(0, 9)], rcv.at[g, pl.ds(OWN, 9)], self_sem)
    keep.start()
    keep.wait()
    for kind, there in ((0, s < spaces - 1), (1, s > 0)):
        @pl.when(there)
        def _():
            for args in sent:
                if args[0] == kind:
                    copy_of(*args, lax.rem(g + groups - args[1], groups)).wait_recv()
    for args in sent:
        if args[0] == 2:
            copy_of(*args, lax.rem(g + groups - args[1], groups)).wait_recv()
    each(lambda kind, args: copy_of(*args, g).wait_send())

    @pl.when(s == 0)
    def _():
        rcv[:, ABOVE:ABOVE + 6] = jnp.zeros((groups, 6) + rcv.shape[2:], F32)

    @pl.when(s == spaces - 1)
    def _():
        rcv[:, BELOW:BELOW + 6] = jnp.zeros((groups, 6) + rcv.shape[2:], F32)


def source_of(row):
    if row < HALF_AZ:
        own = row + 3
        return ABOVE + row, ABOVE + 5, own // 4, own % 4
    if row < HALF_AZ + 8:
        own = row - HALF_AZ
        return OWN + 1 + own, OWN, own // 4, own % 4
    own = row - HALF_AZ - 8
    return BELOW + 1 + own, BELOW, own // 4, own % 4


def window(p):
    suffix = [None] * 8
    suffix[7] = (p[7] + p[8]) + (p[9] + p[10])
    for r in range(6, -1, -1):
        suffix[r] = suffix[r + 1] + p[r]
    out = [suffix[0]]
    prefix = p[11]
    for r in range(1, 8):
        out.append(suffix[r] + prefix)
        if r < 7:
            prefix = prefix + p[11 + r]
    return out


def split(v):
    high = v.astype(BF16).astype(F32)
    return high, v - high


def unpack(rcv, main, tail, wide, groups, dates):
    lane = lax.broadcasted_iota(jnp.int32, (24, LANES), 1)
    for c in range(2):
        for row in range(18):
            plane = source_of(row)[0]
            for l in range(2):
                for h in range(2 * groups):
                    main[c, row, l, pl.ds(dates * h, dates)] = rcv[h % groups, plane, 2 * c + l, 0:dates]
        for n, plane in enumerate((OWN, ABOVE + 5, BELOW)):
            for t in range(2):
                for h in range(2 * groups):
                    wide[c, n, t, pl.ds(dates * h, dates)] = rcv[h % groups, plane, 2 * c + t, 0:dates]
        for row in range(18):
            _, plane, t, q = source_of(row)
            n = (OWN, ABOVE + 5, BELOW).index(plane)
            packed = None
            for b in range(4):
                part = wide[c, n, t, pl.ds(8 * b, 24)]
                if b != q:
                    part = pltpu.roll(part, (32 * (b - q)) % LANES, 1)
                packed = part if packed is None else jnp.where(lane >= 32 * b, part, packed)
            tail[c, row] = packed


def fill_lhs(shift, main, tail, lhs, power_only):
    comps = 1 if power_only else 2
    for l in range(2):
        for b in range(2):
            first, second = [], []
            for row in range(18):
                a = main[0, row, l, pl.ds(16 * b, 16)]
                e = main[1, row, l, pl.ds(16 * b, 16)]
                if power_only:
                    first.append(a * a + e * e)
                else:
                    ao = main[0, row, l, pl.ds(16 * b + shift, 16)]
                    eo = main[1, row, l, pl.ds(16 * b + shift, 16)]
                    first.append(a * ao + e * eo)
                    second.append(e * ao - a * eo)
            for c, planes in enumerate((first, second)[:comps]):
                for r, v in enumerate(window(planes)):
                    high, low = split(v)
                    at = pl.ds(256 * c + 32 * r + 16 * b, 16)
                    lhs[at, LANES * l:LANES * (l + 1)] = high.astype(BF16)
                    lhs[at, LANES * (2 + l):LANES * (3 + l)] = low.astype(BF16)
    first, second = [], []
    for row in range(18):
        a = tail[0, row, 0:8]
        e = tail[1, row, 0:8]
        if power_only:
            first.append(a * a + e * e)
        else:
            ao = tail[0, row, pl.ds(shift, 8)]
            eo = tail[1, row, pl.ds(shift, 8)]
            first.append(a * ao + e * eo)
            second.append(e * ao - a * eo)
    block = lax.broadcasted_iota(jnp.int32, (8, LANES), 1) // 32
    for c, planes in enumerate((first, second)[:comps]):
        for r, v in enumerate(window(planes)):
            for n, part in enumerate(split(v)):
                for b in range(2):
                    both = jnp.concatenate(
                        [jnp.where(block == 2 * b + h, part, 0.0) for h in range(2)], axis=0
                    )
                    lhs[pl.ds(256 * c + 32 * r + 16 * b, 16), LANES * (4 + n):LANES * (5 + n)] = both.astype(BF16)


def pairs(groups, dates, rcv, out, main, tail, wide, lhs, lhs_b, res, res_b, inv, band):
    k = pl.program_id(0)
    total = groups * dates

    @pl.when(k == 0)
    def _():
        i = lax.broadcasted_iota(jnp.int32, (256, 256), 0)
        o = lax.broadcasted_iota(jnp.int32, (256, 256), 1)
        centre = jnp.where((i >= o - HALF_RG) & (i <= o + HALF_RG), 1.0, 0.0).astype(BF16)
        it = lax.broadcasted_iota(jnp.int32, (128, 256), 0) % 32
        ot = lax.broadcasted_iota(jnp.int32, (128, 256), 1)
        col = jnp.where(it < HALF_RG, it - HALF_RG, 256 + it - HALF_RG)
        edge = jnp.where(
            (it < 2 * HALF_RG) & (col >= ot - HALF_RG) & (col <= ot + HALF_RG), 1.0, 0.0
        ).astype(BF16)
        band[0:256] = centre
        band[256:512] = centre
        band[512:640] = edge
        band[640:768] = edge
        unpack(rcv, main, tail, wide, groups, dates)
        fill_lhs(0, main, tail, lhs, True)
        power = jnp.dot(lhs[0:256], band[...], preferred_element_type=F32)
        for l in range(2):
            res[0, l, 0:256] = lax.rsqrt(power[:, LANES * l:LANES * (l + 1)])
        for d in range(total):
            for l in range(2):
                inv[d, :, LANES * l:LANES * (l + 1)] = res[0, l, pl.ds(d, 8, stride=32), :]

    for n, (left, sums) in enumerate(((lhs, res), (lhs_b, res_b))):
        fill_lhs(2 * k + n + 1, main, tail, left, False)
        both = jnp.dot(left[...], band[...], preferred_element_type=F32)
        for c in range(2):
            for l in range(2):
                sums[c, l, 0:256] = both[256 * c:256 * (c + 1), LANES * l:LANES * (l + 1)]
    for n, sums in enumerate((res, res_b)):
        for d in range(total):
            other = lax.rem(d + 2 * k + n + 1, total)
            for l in range(2):
                cols = slice(LANES * l, LANES * (l + 1))
                re = sums[0, l, pl.ds(d, 8, stride=32), :]
                im = sums[1, l, pl.ds(d, 8, stride=32), :]
                out[n, d, :, cols] = jnp.sqrt(re * re + im * im) * (inv[d, :, cols] * inv[other, :, cols])


def body(groups, spaces, stack):
    _, dates, rows, cols = stack.shape
    n_tiles = cols // LANES
    lags = groups * dates // 2
    flat = stack.reshape(2 * dates * rows, cols)
    rcv = pl.pallas_call(
        functools.partial(exchange, groups, spaces, rows, dates),
        out_shape=jax.ShapeDtypeStruct((groups, PLANES, 4, 8, LANES), F32),
        in_specs=[pl.BlockSpec(memory_space=pl.ANY)],
        out_specs=pl.BlockSpec(memory_space=pltpu.VMEM),
        scratch_shapes=[
            pltpu.VMEM((n_tiles, 2 * dates * rows + 16, LANES), F32),
            pltpu.VMEM((groups, 10, 4, 8, LANES), F32),
            pltpu.SemaphoreType.DMA((n_tiles,)),
            pltpu.SemaphoreType.DMA,
            pltpu.SemaphoreType.DMA((3 * groups,)),
            pltpu.SemaphoreType.DMA((3 * groups,)),
        ],
        compiler_params=pltpu.CompilerParams(
            collective_id=0, has_side_effects=True, vmem_limit_bytes=24 << 20
        ),
        name="exchange",
    )(flat)
    width = cols // groups
    return pl.pallas_call(
        functools.partial(pairs, groups, dates),
        grid=(lags // 2,),
        out_shape=jax.ShapeDtypeStruct((lags, groups * dates, rows, width), F32),
        in_specs=[pl.BlockSpec(rcv.shape, lambda k: (0,) * 5)],
        out_specs=pl.BlockSpec((2, groups * dates, rows, width), lambda k: (k, 0, 0, 0)),
        scratch_shapes=[
            pltpu.VMEM((2, 18, 2, 56, LANES), F32),
            pltpu.VMEM((2, 18, 24, LANES), F32),
            pltpu.VMEM((2, 3, 2, 56, LANES), F32),
            pltpu.VMEM((512, 6 * LANES), BF16),
            pltpu.VMEM((512, 6 * LANES), BF16),
            pltpu.VMEM((2, 2, 288, LANES), F32),
            pltpu.VMEM((2, 2, 288, LANES), F32),
            pltpu.VMEM((groups * dates, rows, width), F32),
            pltpu.VMEM((6 * LANES, 256), BF16),
        ],
        compiler_params=pltpu.CompilerParams(vmem_limit_bytes=32 << 20),
        name="pairs",
    )(rcv)


def solution(mesh):
    groups, spaces = mesh.shape["date"], mesh.shape["space"]
    return jax.shard_map(
        functools.partial(body, groups, spaces),
        mesh=mesh,
        in_specs=(P(None, "date", "space", None),),
        out_specs=P(None, None, "space", "date"),
        check_vma=False,
    )
```

```python
import functools

import jax
import jax.numpy as jnp
from jax import lax
from jax.experimental import pallas as pl
from jax.experimental.pallas import tpu as pltpu
from jax.sharding import PartitionSpec as P

F32 = jnp.float32
BF16 = jnp.bfloat16
HALF_AZ = 5
HALF_RG = 11
LANES = 128
MESH = pl.DeviceIdType.MESH
OWN, ABOVE, BELOW = 0, 9, 15
PLANES = 21


def pack_tile(tiles, snd, groups, rows, dates):
    lane = lax.broadcasted_iota(jnp.int32, (8, LANES), 1)

    per = tiles.shape[0] // groups

    def plane(l, c, r):
        return snd[l // per, 1 + r, c * per + l % per]

    for l in range(tiles.shape[0]):
        for c in range(2):
            block = tiles[l, c * dates * rows:(c * dates + 8) * rows].reshape(8, rows, LANES)
            block = jnp.swapaxes(block, 0, 1)
            for r in range(rows):
                snd[l // per, 1 + r, c * per + l % per] = block[r]
    for d in range(groups):
        for c in range(2):
            for t in range(2):
                tail = jnp.zeros((8, LANES), F32)
                for q in range(4):
                    at = 32 * q
                    if d > 0:
                        left = pltpu.roll(plane(d * per - 1, c, 4 * t + q), (at + HALF_RG) % LANES, 1)
                        tail = jnp.where((lane >= at) & (lane < at + HALF_RG), left, tail)
                    if d < groups - 1:
                        right = plane((d + 1) * per, c, 4 * t + q)
                        right = pltpu.roll(right, at + HALF_RG, 1)
                        tail = jnp.where((lane >= at + HALF_RG) & (lane < at + 2 * HALF_RG), right, tail)
                snd[d, 0, 2 * c + t] = tail
                snd[d, 9, 2 * c + t] = tail


def exchange(groups, spaces, rows, dates, x_ref, rcv, tiles, snd, in_sem, self_sem, send_sem, recv_sem):
    g = lax.axis_index("date")
    s = lax.axis_index("space")
    loads = []
    for l in range(tiles.shape[0]):
        n = x_ref.shape[0]
        loads.append(
            pltpu.make_async_copy(
                x_ref.at[:, pl.ds(l * LANES, LANES)], tiles.at[l, pl.ds(0, n)], in_sem.at[l]
            )
        )
        loads[-1].start()
        tiles[l, pl.ds(n, 16)] = jnp.zeros((16, LANES), F32)

    up = lax.rem(s + spaces - 1, spaces)
    down = lax.rem(s + 1, spaces)
    barrier = pltpu.get_barrier_semaphore()

    def greet(d, to):
        pl.semaphore_signal(barrier, inc=1, device_id={"date": d, "space": to}, device_id_type=MESH)

    for off in range(groups):
        d = lax.rem(g + off, groups)
        greet(d, up)
        greet(d, down)
        if off:
            greet(d, s)
    for copy in loads:
        copy.wait()
    pack_tile(tiles, snd, groups, rows, dates)
    pl.semaphore_wait(barrier, 3 * groups - 1)

    def copy_of(kind, off, to, first, count, at, source):
        d = lax.rem(g + off, groups)
        return pltpu.make_async_remote_copy(
            src_ref=snd.at[d, pl.ds(first, count)],
            dst_ref=rcv.at[source, pl.ds(at, count)],
            send_sem=send_sem.at[kind * groups + off],
            recv_sem=recv_sem.at[kind * groups + off],
            device_id={"date": d, "space": to},
            device_id_type=MESH,
        )

    sent = []
    for off in (2, 3, 1, 0):
        sent.append((0, off, up, 0, 6, BELOW))
        sent.append((1, off, down, 4, 6, ABOVE))
        if off:
            sent.append((2, off, s, 0, 9, OWN))
    def each(use):
        for kind, there in ((0, s > 0), (1, s < spaces - 1)):
            @pl.when(there)
            def _():
                for args in sent:
                    if args[0] == kind:
                        use(kind, args)
        for args in sent:
            if args[0] == 2:
                use(2, args)

    each(lambda kind, args: copy_of(*args, g).start())
    keep = pltpu.make_async_copy(snd.at[g, pl.ds(0, 9)], rcv.at[g, pl.ds(OWN, 9)], self_sem)
    keep.start()
    keep.wait()
    for kind, there in ((0, s < spaces - 1), (1, s > 0)):
        @pl.when(there)
        def _():
            for args in sent:
                if args[0] == kind:
                    copy_of(*args, lax.rem(g + groups - args[1], groups)).wait_recv()
    for args in sent:
        if args[0] == 2:
            copy_of(*args, lax.rem(g + groups - args[1], groups)).wait_recv()
    each(lambda kind, args: copy_of(*args, g).wait_send())

    @pl.when(s == 0)
    def _():
        rcv[:, ABOVE:ABOVE + 6] = jnp.zeros((groups, 6) + rcv.shape[2:], F32)

    @pl.when(s == spaces - 1)
    def _():
        rcv[:, BELOW:BELOW + 6] = jnp.zeros((groups, 6) + rcv.shape[2:], F32)


def source_of(row):
    if row < HALF_AZ:
        own = row + 3
        return ABOVE + row, ABOVE + 5, own // 4, own % 4
    if row < HALF_AZ + 8:
        own = row - HALF_AZ
        return OWN + 1 + own, OWN, own // 4, own % 4
    own = row - HALF_AZ - 8
    return BELOW + 1 + own, BELOW, own // 4, own % 4


def window(p):
    suffix = [None] * 8
    suffix[7] = (p[7] + p[8]) + (p[9] + p[10])
    for r in range(6, -1, -1):
        suffix[r] = suffix[r + 1] + p[r]
    out = [suffix[0]]
    prefix = p[11]
    for r in range(1, 8):
        out.append(suffix[r] + prefix)
        if r < 7:
            prefix = prefix + p[11 + r]
    return out


def split(v):
    high = v.astype(BF16).astype(F32)
    return high, v - high


def unpack(rcv, main, tail, wide, groups, dates):
    lane = lax.broadcasted_iota(jnp.int32, (24, LANES), 1)
    for c in range(2):
        for row in range(18):
            plane = source_of(row)[0]
            for l in range(2):
                for h in range(2 * groups):
                    main[c, row, l, pl.ds(dates * h, dates)] = rcv[h % groups, plane, 2 * c + l, 0:dates]
        for n, plane in enumerate((OWN, ABOVE + 5, BELOW)):
            for t in range(2):
                for h in range(2 * groups):
                    wide[c, n, t, pl.ds(dates * h, dates)] = rcv[h % groups, plane, 2 * c + t, 0:dates]
        for row in range(18):
            _, plane, t, q = source_of(row)
            n = (OWN, ABOVE + 5, BELOW).index(plane)
            packed = None
            for b in range(4):
                part = wide[c, n, t, pl.ds(8 * b, 24)]
                if b != q:
                    part = pltpu.roll(part, (32 * (b - q)) % LANES, 1)
                packed = part if packed is None else jnp.where(lane >= 32 * b, part, packed)
            tail[c, row] = packed


def fill_lhs(shift, main, tail, lhs, power_only):
    comps = 1 if power_only else 2
    for l in range(2):
        for b in range(2):
            first, second = [], []
            for row in range(18):
                a = main[0, row, l, pl.ds(16 * b, 16)]
                e = main[1, row, l, pl.ds(16 * b, 16)]
                if power_only:
                    first.append(a * a + e * e)
                else:
                    ao = main[0, row, l, pl.ds(16 * b + shift, 16)]
                    eo = main[1, row, l, pl.ds(16 * b + shift, 16)]
                    first.append(a * ao + e * eo)
                    second.append(e * ao - a * eo)
            for c, planes in enumerate((first, second)[:comps]):
                for r, v in enumerate(window(planes)):
                    high, low = split(v)
                    at = pl.ds(256 * c + 32 * r + 16 * b, 16)
                    lhs[at, LANES * l:LANES * (l + 1)] = high.astype(BF16)
                    lhs[at, LANES * (2 + l):LANES * (3 + l)] = low.astype(BF16)
    first, second = [], []
    for row in range(18):
        a = tail[0, row, 0:8]
        e = tail[1, row, 0:8]
        if power_only:
            first.append(a * a + e * e)
        else:
            ao = tail[0, row, pl.ds(shift, 8)]
            eo = tail[1, row, pl.ds(shift, 8)]
            first.append(a * ao + e * eo)
            second.append(e * ao - a * eo)
    block = lax.broadcasted_iota(jnp.int32, (8, LANES), 1) // 32
    for c, planes in enumerate((first, second)[:comps]):
        for r, v in enumerate(window(planes)):
            for n, part in enumerate(split(v)):
                for b in range(2):
                    both = jnp.concatenate(
                        [jnp.where(block == 2 * b + h, part, 0.0) for h in range(2)], axis=0
                    )
                    lhs[pl.ds(256 * c + 32 * r + 16 * b, 16), LANES * (4 + n):LANES * (5 + n)] = both.astype(BF16)


def pairs(groups, dates, rcv, out, main, tail, wide, lhs, lhs_b, res, res_b, inv, band):
    k = pl.program_id(0)
    total = groups * dates

    @pl.when(k == 0)
    def _():
        i = lax.broadcasted_iota(jnp.int32, (256, 256), 0)
        o = lax.broadcasted_iota(jnp.int32, (256, 256), 1)
        centre = jnp.where((i >= o - HALF_RG) & (i <= o + HALF_RG), 1.0, 0.0).astype(BF16)
        it = lax.broadcasted_iota(jnp.int32, (128, 256), 0) % 32
        ot = lax.broadcasted_iota(jnp.int32, (128, 256), 1)
        col = jnp.where(it < HALF_RG, it - HALF_RG, 256 + it - HALF_RG)
        edge = jnp.where(
            (it < 2 * HALF_RG) & (col >= ot - HALF_RG) & (col <= ot + HALF_RG), 1.0, 0.0
        ).astype(BF16)
        band[0:256] = centre
        band[256:512] = centre
        band[512:640] = edge
        band[640:768] = edge
        unpack(rcv, main, tail, wide, groups, dates)
        fill_lhs(0, main, tail, lhs, True)
        power = jnp.dot(lhs[0:256], band[...], preferred_element_type=F32)
        for l in range(2):
            res[0, l, 0:256] = lax.rsqrt(power[:, LANES * l:LANES * (l + 1)])
        for d in range(total):
            for l in range(2):
                inv[d, :, LANES * l:LANES * (l + 1)] = res[0, l, pl.ds(d, 8, stride=32), :]

    for n, (left, sums) in enumerate(((lhs, res), (lhs_b, res_b))):
        fill_lhs(2 * k + n + 1, main, tail, left, False)
        both = jnp.dot(left[...], band[...], preferred_element_type=F32)
        for c in range(2):
            for l in range(2):
                sums[c, l, 0:256] = both[256 * c:256 * (c + 1), LANES * l:LANES * (l + 1)]
    for n, sums in enumerate((res, res_b)):
        for d in range(total):
            other = lax.rem(d + 2 * k + n + 1, total)
            for l in range(2):
                cols = slice(LANES * l, LANES * (l + 1))
                re = sums[0, l, pl.ds(d, 8, stride=32), :]
                im = sums[1, l, pl.ds(d, 8, stride=32), :]
                out[n, d, :, cols] = jnp.sqrt(re * re + im * im) * (inv[d, :, cols] * inv[other, :, cols])


def body(groups, spaces, stack):
    _, dates, rows, cols = stack.shape
    n_tiles = cols // LANES
    lags = groups * dates // 2
    flat = stack.reshape(2 * dates * rows, cols)
    rcv = pl.pallas_call(
        functools.partial(exchange, groups, spaces, rows, dates),
        out_shape=jax.ShapeDtypeStruct((groups, PLANES, 4, 8, LANES), F32),
        in_specs=[pl.BlockSpec(memory_space=pltpu.HBM)],
        out_specs=pl.BlockSpec(memory_space=pltpu.VMEM),
        scratch_shapes=[
            pltpu.VMEM((n_tiles, 2 * dates * rows + 16, LANES), F32),
            pltpu.VMEM((groups, 10, 4, 8, LANES), F32),
            pltpu.SemaphoreType.DMA((n_tiles,)),
            pltpu.SemaphoreType.DMA,
            pltpu.SemaphoreType.DMA((3 * groups,)),
            pltpu.SemaphoreType.DMA((3 * groups,)),
        ],
        compiler_params=pltpu.CompilerParams(
            collective_id=0, has_side_effects=True, vmem_limit_bytes=24 << 20
        ),
        name="exchange",
    )(flat)
    width = cols // groups
    return pl.pallas_call(
        functools.partial(pairs, groups, dates),
        grid=(lags // 2,),
        out_shape=jax.ShapeDtypeStruct((lags, groups * dates, rows, width), F32),
        in_specs=[pl.BlockSpec(rcv.shape, lambda k: (0,) * 5)],
        out_specs=pl.BlockSpec((2, groups * dates, rows, width), lambda k: (k, 0, 0, 0)),
        scratch_shapes=[
            pltpu.VMEM((2, 18, 2, 56, LANES), F32),
            pltpu.VMEM((2, 18, 24, LANES), F32),
            pltpu.VMEM((2, 3, 2, 56, LANES), F32),
            pltpu.VMEM((512, 6 * LANES), BF16),
            pltpu.VMEM((512, 6 * LANES), BF16),
            pltpu.VMEM((2, 2, 288, LANES), F32),
            pltpu.VMEM((2, 2, 288, LANES), F32),
            pltpu.VMEM((groups * dates, rows, width), F32),
            pltpu.VMEM((6 * LANES, 256), BF16),
        ],
        compiler_params=pltpu.CompilerParams(vmem_limit_bytes=32 << 20),
        name="pairs",
    )(rcv)


def solution(mesh):
    groups, spaces = mesh.shape["date"], mesh.shape["space"]
    return jax.shard_map(
        functools.partial(body, groups, spaces),
        mesh=mesh,
        in_specs=(P(None, "date", "space", None),),
        out_specs=P(None, None, "space", "date"),
        check_vma=False,
    )
```
